32 devices in a mesh: groups: 2 (over x), seq: 8 (over z, y), chan: 2 (over core).
Axes of the slice: x: 2, y: 2, z: 4, core: 2. Of those that a mesh axis runs over, the one named last changes fastest.
Arguments:
- residual_input_stream: bfloat16 [2048, 2048], P(('groups', 'seq'), 'chan'), parts along dimension 0, may hold values from -6 to 6
- nucleotide_index: int32 [2048], P(('groups', 'seq')), parts along dimension 0, may hold values from 0 to 3
- nucleotide_embedding: bfloat16 [4, 2048], replicated, may hold values from -6 to 6
- mixing_weight_half: bfloat16 [2048, 4096], P('chan'), may hold values from -0.125 to 0.125
- short_tap_kernel: float32 [7, 2048], replicated, may hold values from -2.5 to 2.5
- dilated_tap_kernel: float32 [5, 2048], replicated, may hold values from -2.5 to 2.5
- dilations: int32 [16], replicated, may hold values from 1 to 16, as said below
- cotangent: bfloat16 [2048, 2048], P(('groups', 'seq'), 'chan'), parts along dimension 0, may hold values from -6 to 6
Outputs:
- block_result_output: bfloat16 [2048, 2048], P(('groups', 'seq'), 'chan'), parts along dimension 0
- hidden_input_gradient: float32 [2048, 2048], P(('groups', 'seq'), 'chan'), parts along dimension 0
- mixing_half_gradient: float32 [4096, 4096], P(('groups', 'chan'), 'seq'), parts along dimension 0
- embedding_table_gradient: float32 [8, 2048], P('groups'), parts along dimension 0
- short_kernel_gradient: float32 [14, 2048], P('groups'), parts along dimension 0
- dilated_kernel_gradient: float32 [10, 2048], P('groups'), parts along dimension 0
The draws below stay inside these ranges and needn't reach their ends.
There are 2 independent parts, one for each index of `groups`. The reference program is written for one: setup_inputs(seed, part) draws one part's arguments, and reference() takes and returns one part's arrays. A program takes and returns all parts, laid end to end along the dimension named above; an argument that names none is the same for every part. Nothing has to cross between parts.
Inputs may be any that keep to these rules, and one draw needn't show every extreme that they name: `dilations`: some group has dilation 16 and some group has dilation 1.
All inputs are finite; a program needn't handle non-finite values.
Results may differ from the reference program's by a relative error of at most 0.014.
Values may be sent and summed in bfloat16 or wider, within the bound.
A program may use at most 128 MiB of HBM per device.

```python
import jax
import jax.numpy as jnp
from jax import lax

MODEL_WIDTH = 2048
DH = 1024
GW = 128
GROUPS = 16
TOK_DEV = 128
DMAX = 16
TOKENS = 1024
N_SEQ = 8


def draw_dilations(key, part):
    values = jax.random.randint(jax.random.fold_in(key, 11), (GROUPS,), 1, DMAX + 1, dtype=jnp.int32)
    chosen_order = jax.random.permutation(jax.random.fold_in(key, 12), GROUPS)
    values = values.at[chosen_order[0]].set(DMAX)
    values = values.at[chosen_order[1]].set(1)
    return values.astype(jnp.int32)


def with_ends(array, own_key, low, high):
    dims = array.shape
    place = [jax.random.randint(jax.random.fold_in(own_key, axis), (), 0, dims[axis]) for axis in range(len(dims))]
    array = array.at[tuple(place)].set(low)
    longest = dims.index(max(dims))
    place[longest] = (place[longest] + 1) % dims[longest]
    return array.at[tuple(place)].set(high)


def shard_levels(own_key, shape, cuts, smallest, largest):
    factor_of = 1.0
    for position, shards_of in cuts:
        steps = jax.random.uniform(jax.random.fold_in(jax.random.fold_in(own_key, 6), position), (shards_of,), jnp.float32, smallest / len(cuts), largest / len(cuts))
        factor_of = factor_of * jnp.repeat(jnp.exp(steps), shape[position] // shards_of).reshape((-1,) + (1,) * (len(shape) - 1 - position))
    return factor_of


def noise(own_key, extent, spread, most, cuts=(), held_as=jnp.bfloat16):
    loudness = shard_levels(own_key, extent, cuts, -0.22, 0.18) if cuts else 1.0
    drawn = jax.random.normal(own_key, extent, jnp.float32) * spread * loudness
    return jnp.minimum(jnp.maximum(drawn, -most), most).astype(held_as)


def setup_inputs(seed: int = 0, part: int = 0) -> dict:
    keys = jax.random.split(jax.random.key(seed), 9)
    part_splits = jax.random.split(jax.random.fold_in(keys[8], part), 9)
    return {
        "residual_input_stream": noise(part_splits[0], (TOKENS, MODEL_WIDTH), 1.0, 6.0, ((0, 8), (1, 2))),
        "nucleotide_index": with_ends(jax.random.randint(part_splits[1], (TOKENS,), 0, 4), jax.random.fold_in(part_splits[1], 1), 0, 3).astype(jnp.int32),
        "nucleotide_embedding": noise(keys[2], (4, MODEL_WIDTH), 1.0, 6.0),
        "mixing_weight_half": noise(keys[3], (MODEL_WIDTH, 4 * DH), MODEL_WIDTH ** -0.5, 0.125, ((0, 2),)),
        "short_tap_kernel": noise(keys[4], (7, MODEL_WIDTH), 0.3, 2.5, (), jnp.float32),
        "dilated_tap_kernel": noise(keys[5], (5, MODEL_WIDTH), 0.3, 2.5, (), jnp.float32),
        "dilations": draw_dilations(jax.random.fold_in(keys[8], 71), part),
        "cotangent": noise(part_splits[7], (TOKENS, MODEL_WIDTH), 1.0, 6.0, ((0, 8), (1, 2))),
    }


def rounded_half_value(values):
    return lax.optimization_barrier(values.astype(jnp.bfloat16)).astype(jnp.float32)


def flip_sequence_channels(values):
    return values[::-1, ::-1]


def short_taps(values, kernel, facing):
    length = values.shape[0]
    padded = jnp.pad(values, ((3, 3), (0, 0)))
    return sum(kernel[t] * padded[3 + facing * (t - 3):3 + facing * (t - 3) + length] for t in range(7))


def short_corr(values, source):
    length = values.shape[0]
    padded = jnp.pad(source, ((3, 3), (0, 0)))
    return jnp.stack([jnp.sum(values * padded[t:t + length], axis=0) for t in range(7)])


def dilated_view(padded, dilations, offset, length):
    grouped = padded.reshape(padded.shape[0], -1, GW)

    def pick(column, stride):
        first_row = (2 * DMAX + offset * stride).astype(jnp.int32)
        return lax.dynamic_slice_in_dim(column, first_row, length, 0)

    return jax.vmap(pick, in_axes=(1, 0), out_axes=1)(grouped, dilations).reshape(length, -1)


def dilated_response(values, kernel, dilations, facing):
    length = values.shape[0]
    padded = jnp.pad(values, ((2 * DMAX, 2 * DMAX), (0, 0)))
    return sum(kernel[t] * dilated_view(padded, dilations, facing * (t - 2), length) for t in range(5))


def dilated_correlation(values, source, dilations):
    length = values.shape[0]
    padded = jnp.pad(source, ((2 * DMAX, 2 * DMAX), (0, 0)))
    return jnp.stack([jnp.sum(values * dilated_view(padded, dilations, t - 2, length), axis=0) for t in range(5)])


def reference(residual_input_stream, nucleotide_index, nucleotide_embedding, mixing_weight_half, short_tap_kernel, dilated_tap_kernel, dilations, cotangent):
    length = residual_input_stream.shape[0]
    half_model_width = MODEL_WIDTH // 2
    onehot = (nucleotide_index[:, None] == jnp.arange(4, dtype=jnp.int32)[None, :]).astype(jnp.float32)
    hidden = (residual_input_stream.astype(jnp.float32) + jnp.dot(onehot, nucleotide_embedding.astype(jnp.float32), precision=lax.Precision.HIGHEST)).astype(jnp.bfloat16)
    halves = mixing_weight_half.reshape(MODEL_WIDTH, 4, half_model_width)
    mixing = jnp.concatenate([halves, halves[::-1, :, ::-1]], axis=2).reshape(MODEL_WIDTH, 4 * MODEL_WIDTH)
    streams = jnp.dot(hidden, mixing, preferred_element_type=jnp.float32).astype(jnp.bfloat16)
    short_in, long_branch_input, short_gate, long_gate = [streams[:, k * MODEL_WIDTH:(k + 1) * MODEL_WIDTH].astype(jnp.float32) for k in range(4)]
    tied_short = short_tap_kernel + short_tap_kernel[::-1, ::-1]
    short_out = short_taps(short_in, tied_short, 1)
    forward_strand_path = dilated_response(long_branch_input, dilated_tap_kernel, dilations, 1)
    reverse_strand_path = rounded_half_value(flip_sequence_channels(dilated_response(flip_sequence_channels(long_branch_input), dilated_tap_kernel, dilations, 1)))
    long_out = forward_strand_path + reverse_strand_path
    block_result_output = (hidden.astype(jnp.float32) + short_gate * short_out + long_gate * long_out).astype(jnp.bfloat16)
    upstream = cotangent.astype(jnp.float32)
    short_grad = upstream * short_gate
    long_branch_gradient = rounded_half_value(upstream * long_gate)
    d_short_in = short_taps(short_grad, tied_short, -1)
    reverse_strand_backward = rounded_half_value(flip_sequence_channels(dilated_response(flip_sequence_channels(long_branch_gradient), dilated_tap_kernel, dilations, -1)))
    long_input_gradient = dilated_response(long_branch_gradient, dilated_tap_kernel, dilations, -1) + reverse_strand_backward
    stream_grads = jnp.concatenate([d_short_in, long_input_gradient, upstream * short_out, upstream * long_out], axis=1).astype(jnp.bfloat16)
    hidden_input_gradient = upstream + lax.dot_general(stream_grads, mixing, (((1,), (1,)), ((), ())), preferred_element_type=jnp.float32)
    grad_blocks = stream_grads.reshape(length, 4, MODEL_WIDTH)
    lower_half = grad_blocks[:, :, :half_model_width].reshape(N_SEQ, TOK_DEV, 4 * half_model_width)
    upper_half = grad_blocks[:, :, half_model_width:][:, :, ::-1].reshape(N_SEQ, TOK_DEV, 4 * half_model_width)
    forward_rows = hidden.reshape(N_SEQ, TOK_DEV, MODEL_WIDTH)
    turned_rows = hidden[:, ::-1].reshape(N_SEQ, TOK_DEV, MODEL_WIDTH)

    def add_block(running, pieces):
        straight, turned, low_part, high_part = pieces
        block_term = lax.dot_general(straight, low_part, (((0,), (0,)), ((), ())), preferred_element_type=jnp.float32)
        block_term = block_term + lax.dot_general(turned, high_part, (((0,), (0,)), ((), ())), preferred_element_type=jnp.float32)
        return running + rounded_half_value(block_term), None

    mixing_half_gradient = lax.scan(add_block, jnp.zeros((MODEL_WIDTH, 4 * half_model_width), jnp.float32), (forward_rows, turned_rows, lower_half, upper_half))[0]
    embedding_table_gradient = jnp.dot(onehot.T, hidden_input_gradient, precision=lax.Precision.HIGHEST)
    raw_short = short_corr(short_grad, short_in)
    short_kernel_gradient = raw_short + raw_short[::-1, ::-1]
    dilated_kernel_gradient = dilated_correlation(long_branch_gradient, long_branch_input, dilations) + dilated_correlation(flip_sequence_channels(long_branch_gradient), flip_sequence_channels(long_branch_input), dilations)
    return (block_result_output, hidden_input_gradient, mixing_half_gradient, embedding_table_gradient, short_kernel_gradient, dilated_kernel_gradient)
```

```python
import functools

import jax
import jax.numpy as jnp
from jax import lax
from jax.experimental import pallas as pl
from jax.experimental.pallas import tpu as pltpu
from jax.sharding import PartitionSpec as P

GW = 128
DMAX = 16
MARGIN = 2 * DMAX
F32 = jnp.float32
BF16 = jnp.bfloat16
MESH = pl.DeviceIdType.MESH


def swap(value):
    return lax.ppermute(value, "chan", [(0, 1), (1, 0)])


def mm(a, b):
    return jnp.dot(a, b, preferred_element_type=F32)


def mm_t(a, b):
    return lax.dot_general(a, b, (((1,), (1,)), ((), ())), preferred_element_type=F32)


def rounded(v):
    return v.astype(BF16).astype(F32)


def seq_kernel(fd_ref, md_ref, tied_ref, kf_ref, km_ref, cur_ref, prev_ref, next_ref, cot_ref,
               cprev_ref, cnext_ref, hid_ref, out_ref, sg_ref, corr_ref, si, li, gs, gl):
    length, width = cot_ref.shape
    corr_ref[...] = jnp.zeros_like(corr_ref)

    def group(g, carry):
        def cols(s):
            return pl.ds(pl.multiple_of(s * width + g * GW, GW), GW)

        own = cols(0)

        def rows3(a, b, c, s):
            return (a[:, cols(s)].astype(F32), b[:, cols(s)].astype(F32), c[:, cols(s)].astype(F32))

        def fill(buf, parts):
            buf[0:MARGIN, :] = parts[0]
            buf[MARGIN:MARGIN + length, :] = parts[1]
            buf[MARGIN + length:, :] = parts[2]

        cots = rows3(cprev_ref, cot_ref, cnext_ref, 0)
        fill(si, rows3(prev_ref, cur_ref, next_ref, 0))
        fill(li, rows3(prev_ref, cur_ref, next_ref, 1))
        sgate = rows3(prev_ref, cur_ref, next_ref, 2)
        lgate = rows3(prev_ref, cur_ref, next_ref, 3)
        sgrad = [c * v for c, v in zip(cots, sgate)]
        lgrad = [rounded(c * v) for c, v in zip(cots, lgate)]
        fill(gs, sgrad)
        fill(gl, lgrad)
        fd, md = fd_ref[g], md_ref[g]
        cot = cots[1]
        short_out = jnp.zeros((length, GW), F32)
        d_short = jnp.zeros((length, GW), F32)
        for t in range(7):
            tap = tied_ref[t:t + 1, own]
            view = si[MARGIN + t - 3:MARGIN + t - 3 + length, :]
            short_out += tap * view
            corr_ref[t:t + 1, own] = jnp.sum(sgrad[1] * view, axis=0, keepdims=True)
            d_short += tap * gs[MARGIN - t + 3:MARGIN - t + 3 + length, :]
        fwd = jnp.zeros((length, GW), F32)
        bwd = jnp.zeros((length, GW), F32)
        mir = jnp.zeros((length, GW), F32)
        mirb = jnp.zeros((length, GW), F32)
        for t in range(5):
            kf = kf_ref[t:t + 1, own]
            km = km_ref[t:t + 1, own]
            view = li[pl.ds(MARGIN + (t - 2) * fd, length), :]
            fwd += kf * view
            corr_ref[7 + t:8 + t, own] = jnp.sum(lgrad[1] * view, axis=0, keepdims=True)
            view = li[pl.ds(MARGIN - (t - 2) * md, length), :]
            mir += km * view
            corr_ref[12 + t:13 + t, own] = jnp.sum(lgrad[1] * view, axis=0, keepdims=True)
            bwd += kf * gl[pl.ds(MARGIN - (t - 2) * fd, length), :]
            mirb += km * gl[pl.ds(MARGIN + (t - 2) * md, length), :]
        long_out = fwd + rounded(mir)
        out_ref[:, own] = (
            hid_ref[:, own].astype(F32) + sgate[1] * short_out + lgate[1] * long_out
        ).astype(BF16)
        sg_ref[:, cols(0)] = d_short.astype(BF16)
        sg_ref[:, cols(1)] = (bwd + rounded(mirb)).astype(BF16)
        sg_ref[:, cols(2)] = (cot * short_out).astype(BF16)
        sg_ref[:, cols(3)] = (cot * long_out).astype(BF16)
        return carry

    lax.fori_loop(0, width // GW, group, 0)


def col_kernel(meta_ref, fd_ref, md_ref, tied_ref, kf_ref, km_ref, x_ref, cot_ref, sg_ref, buf):
    length, width = cot_ref.shape
    stream = meta_ref[0]
    step = 128
    buf[0:MARGIN, :] = jnp.zeros((MARGIN, GW), F32)
    buf[MARGIN + length:, :] = jnp.zeros((MARGIN, GW), F32)

    def run(back, short, g):
        own = pl.ds(pl.multiple_of(g * GW, GW), GW)
        sign = -1 if back else 1

        def load(i, carry):
            at = pl.multiple_of(i * step, step)
            v = x_ref[pl.ds(at, step), own].astype(F32)
            if back:
                v = v * cot_ref[pl.ds(at, step), own].astype(F32)
                if not short:
                    v = rounded(v)
            buf[pl.ds(at + MARGIN, step), :] = v
            return carry

        lax.fori_loop(0, length // step, load, 0)
        fd, md = fd_ref[g], md_ref[g]

        def body(i, carry):
            at = pl.multiple_of(i * step, step)
            base = at + MARGIN
            acc = jnp.zeros((step, GW), F32)
            if short:
                for t in range(7):
                    acc += tied_ref[t:t + 1, own] * buf[pl.ds(base + sign * (t - 3), step), :]
            else:
                mir = jnp.zeros((step, GW), F32)
                for t in range(5):
                    acc += kf_ref[t:t + 1, own] * buf[pl.ds(base + sign * (t - 2) * fd, step), :]
                    mir += km_ref[t:t + 1, own] * buf[pl.ds(base - sign * (t - 2) * md, step), :]
                acc += rounded(mir)
            if not back:
                acc = acc * cot_ref[pl.ds(at, step), own].astype(F32)
            sg_ref[pl.ds(at, step), own] = acc.astype(BF16)
            return carry

        lax.fori_loop(0, length // step, body, 0)

    def group(g, carry):
        for s in range(4):
            pl.when(stream == s)(functools.partial(run, s < 2, s % 2 == 0, g))
        return carry

    lax.fori_loop(0, width // GW, group, 0)


def sum_kernel(count, x_ref, o_ref, got, mine, full, ssem, rsem, bssem, brsem):
    me = lax.axis_index("seq")
    chan = lax.axis_index("chan")
    part = lax.axis_index("groups")
    peers = [(d, c) for d in range(count) for c in range(2) if d or c]

    def device(d, c):
        return (part, lax.rem(me + d, count), lax.rem(chan + c, 2))

    barrier = pltpu.get_barrier_semaphore()
    for d, c in peers:
        pl.semaphore_signal(barrier, inc=1, device_id=device(d, c), device_id_type=MESH)
    pl.semaphore_wait(barrier, len(peers))
    sends = []
    for d in range(1, count):
        copy = pltpu.make_async_remote_copy(
            src_ref=x_ref.at[lax.rem(me + d, count)],
            dst_ref=got.at[d],
            send_sem=ssem.at[d],
            recv_sem=rsem.at[d],
            device_id=device(d, 0),
            device_id_type=MESH,
        )
        copy.start()
        sends.append(copy)
    total = x_ref[me]
    for d in range(1, count):
        sends[d - 1].wait_recv()
        total = total + got[d]
    mine[...] = total
    casts = []
    for d, c in peers:
        copy = pltpu.make_async_remote_copy(
            src_ref=mine,
            dst_ref=full.at[chan, me],
            send_sem=bssem.at[d, c],
            recv_sem=brsem.at[d, c],
            device_id=device(d, c),
            device_id_type=MESH,
        )
        copy.start()
        casts.append(copy)
    full[chan, me] = total
    for copy in casts:
        copy.wait_recv()
    o_ref[...] = full[...]
    for copy in sends + casts:
        copy.wait_send()


def vmem():
    return pl.BlockSpec(memory_space=pltpu.VMEM)


def smem():
    return pl.BlockSpec(memory_space=pltpu.SMEM)


def all_sum(values, count):
    rows, width = values.shape
    lines = rows * width // (count * 128)
    x = values.reshape(count, lines, 128)
    out = pl.pallas_call(
        functools.partial(sum_kernel, count),
        out_shape=jax.ShapeDtypeStruct((2, count, lines, 128), F32),
        in_specs=[vmem()],
        out_specs=vmem(),
        scratch_shapes=[
            pltpu.VMEM((count, lines, 128), F32),
            pltpu.VMEM((lines, 128), F32),
            pltpu.VMEM((2, count, lines, 128), F32),
            pltpu.SemaphoreType.DMA((count,)),
            pltpu.SemaphoreType.DMA((count,)),
            pltpu.SemaphoreType.DMA((count, 2)),
            pltpu.SemaphoreType.DMA((count, 2)),
        ],
        compiler_params=pltpu.CompilerParams(collective_id=0, has_side_effects=True),
        cost_estimate=pl.CostEstimate(flops=10**6, bytes_accessed=10**6, transcendentals=0),
    )(x)
    return out.reshape(2, rows, width)


def local(residual, index, table, weight, short_taps, long_taps, dilations, cotangent):
    length, width = residual.shape
    groups = width // GW
    count = lax.axis_size("seq")
    side = lax.axis_index("chan")
    me = lax.axis_index("seq")
    low = side == 0
    own_table = lax.dynamic_slice_in_dim(table, side * width, width, 1).astype(F32)
    picked = sum(jnp.where(index[:, None] == b, own_table[b:b + 1], 0.0) for b in range(4))
    hidden = (residual.astype(F32) + picked).astype(BF16)

    at = jnp.arange(width, dtype=jnp.int32)
    total = at[:, None] + at[None, :]
    anti = total == width - 1
    turn = anti.astype(BF16)
    order = jnp.where(low, at[:, None] == at[None, :], anti).astype(BF16)

    short_low, short_high = short_taps[:, :width], short_taps[:, ::-1][:, :width]
    tied = jnp.where(low, short_low + short_high[::-1], short_high + short_low[::-1])
    long_low, long_high = long_taps[:, :width], long_taps[:, ::-1][:, :width]
    kf, km = jnp.where(low, long_low, long_high), jnp.where(low, long_high, long_low)
    dil_low, dil_high = dilations[:groups], dilations[::-1][:groups]
    fd, md = jnp.where(low, dil_low, dil_high), jnp.where(low, dil_high, dil_low)

    cot = mm(cotangent, order).astype(BF16)
    all_hidden = lax.all_gather(hidden, "seq", axis=0, tiled=True)
    all_cot = lax.all_gather(cot, "seq", axis=0, tiled=True)

    turned = mm(swap(hidden), turn).astype(BF16)
    hid = mm(hidden, order).astype(BF16)
    far = mm(jnp.where(low, turned, hidden), weight).astype(BF16)
    near = mm(jnp.where(low, hidden, turned), weight)
    streams = (near + swap(far).astype(F32)).astype(BF16)

    up = [(i, i + 1) for i in range(count - 1)]
    down = [(i + 1, i) for i in range(count - 1)]
    prev = lax.ppermute(streams[length - MARGIN:], "seq", up)
    nxt = lax.ppermute(streams[:MARGIN], "seq", down)
    cprev = lax.ppermute(cot[length - MARGIN:], "seq", up)
    cnext = lax.ppermute(cot[:MARGIN], "seq", down)
    span = length + 2 * MARGIN
    block, sg, corr = pl.pallas_call(
        seq_kernel,
        out_shape=(
            jax.ShapeDtypeStruct((length, width), BF16),
            jax.ShapeDtypeStruct((length, 4 * width), BF16),
            jax.ShapeDtypeStruct((17, width), F32),
        ),
        in_specs=[smem()] * 2 + [vmem()] * 10,
        out_specs=(vmem(),) * 3,
        scratch_shapes=[pltpu.VMEM((span, GW), F32)] * 4,
        compiler_params=pltpu.CompilerParams(vmem_limit_bytes=32 * 2**20),
        cost_estimate=pl.CostEstimate(flops=10**7, bytes_accessed=2 * 10**7, transcendentals=0),
    )(fd, md, tied, kf, km, streams, prev, nxt, cot, cprev, cnext, hid)
    block_result_output = mm(block, order).astype(BF16)

    other_sg = swap(sg)
    sg0, sg1 = jnp.where(low, sg, other_sg), jnp.where(low, other_sg, sg)
    far = mm_t(sg1, weight).astype(BF16)
    near = mm_t(sg0, weight)
    hidden_input_gradient = cotangent.astype(F32) + near + mm(swap(far), turn)

    embedding = jnp.stack(
        [
            jnp.sum(jnp.where(index[:, None] == b, hidden_input_gradient, 0.0), axis=0)
            for b in range(4)
        ]
    )
    small = jnp.concatenate([corr, embedding, jnp.zeros((3, width), F32)], axis=0)
    summed = all_sum(small, count)

    cw = weight.shape[1] // count
    per = count // 4
    stream = me // per
    first = lax.rem(me, per) * cw
    source = lax.rem(me + count // 2, count) * cw
    all_turned = mm(swap(all_hidden), turn).astype(BF16)
    columns = lax.dynamic_slice_in_dim(weight, source, cw, 1)
    far = mm(jnp.where(low, all_turned, all_hidden), columns).astype(BF16)
    near = mm(jnp.where(low, all_hidden, all_turned), columns)
    values = (near + swap(far).astype(F32)).astype(BF16)

    def here(v):
        return lax.dynamic_slice_in_dim(v, first, cw, 1)

    col_sg = pl.pallas_call(
        col_kernel,
        out_shape=jax.ShapeDtypeStruct(values.shape, BF16),
        in_specs=[smem()] * 3 + [vmem()] * 5,
        out_specs=vmem(),
        scratch_shapes=[pltpu.VMEM((values.shape[0] + 2 * MARGIN, GW), F32)],
        compiler_params=pltpu.CompilerParams(vmem_limit_bytes=32 * 2**20),
        cost_estimate=pl.CostEstimate(flops=10**7, bytes_accessed=10**7, transcendentals=0),
    )(
        stream.reshape(1),
        lax.dynamic_slice_in_dim(fd, first // GW, cw // GW, 0),
        lax.dynamic_slice_in_dim(md, first // GW, cw // GW, 0),
        here(tied),
        here(kf),
        here(km),
        values,
        here(all_cot),
    )
    other = swap(col_sg)
    rows = (((0,), (0,)), ((), ()))
    mixing_half_gradient = lax.dot_general(
        all_hidden, jnp.where(low, col_sg, other), rows, preferred_element_type=F32
    ) + lax.dot_general(
        all_turned, jnp.where(low, other, col_sg), rows, preferred_element_type=F32
    )

    a, b = summed[0], summed[1]
    tied_sum = a[0:7] + b[0:7][::-1]
    short_kernel_gradient = jnp.concatenate([tied_sum, tied_sum[::-1, ::-1]], axis=1)
    dilated_kernel_gradient = jnp.concatenate(
        [a[7:12] + b[12:17], (b[7:12] + a[12:17])[:, ::-1]], axis=1
    )
    embedding_table_gradient = jnp.concatenate([a[17:21], b[17:21]], axis=1)
    return (
        block_result_output,
        hidden_input_gradient,
        mixing_half_gradient,
        embedding_table_gradient,
        short_kernel_gradient,
        dilated_kernel_gradient,
    )


def solution(mesh):
    placed = (
        P(("groups", "seq"), "chan"),
        P(("groups", "seq")),
        P(),
        P("chan", None),
        P(),
        P(),
        P(),
        P(("groups", "seq"), "chan"),
    )
    return jax.shard_map(
        local,
        mesh=mesh,
        in_specs=placed,
        out_specs=(
            P(("groups", "seq"), "chan"),
            P(("groups", "seq"), "chan"),
            P(("groups", "chan"), "seq"),
            P("groups", None),
            P("groups", None),
            P("groups", None),
        ),
        check_vma=False,
    )
```

```python
import functools

import jax
import jax.numpy as jnp
from jax import lax
from jax.experimental import pallas as pl
from jax.experimental.pallas import tpu as pltpu
from jax.sharding import PartitionSpec as P

GW = 128
DMAX = 16
MARGIN = 2 * DMAX
F32 = jnp.float32
BF16 = jnp.bfloat16
MESH = pl.DeviceIdType.MESH


def swap(value):
    return lax.ppermute(value, "chan", [(0, 1), (1, 0)])


def mm(a, b):
    return jnp.dot(a, b, preferred_element_type=F32)


def mm_t(a, b):
    return lax.dot_general(a, b, (((1,), (1,)), ((), ())), preferred_element_type=F32)


def rounded(v):
    return v.astype(BF16).astype(F32)


def seq_kernel(count, fd_ref, md_ref, tied_ref, kf_ref, km_ref, cur_ref, cot_ref, hid_ref, w_ref,
               out_ref, corr_ref, near_ref, got_ref, col_ref, si, li, gs, gl, prev_ref, next_ref,
               cprev_ref, cnext_ref, stack, wbuf, far, got, landed, wsem, hsend, hrecv, asend,
               arecv, psend, precv):
    length, width = cot_ref.shape
    cw = 4 * width // count
    me = lax.axis_index("seq")
    chan = lax.axis_index("chan")
    part = lax.axis_index("groups")
    load = pltpu.make_async_copy(w_ref, wbuf, wsem)
    load.start()

    def device(d, c):
        return (part, lax.rem(me + d, count), lax.rem(chan + c, 2))

    barrier = pltpu.get_barrier_semaphore()
    for d in range(count):
        pl.semaphore_signal(barrier, inc=1, device_id=device(d, 0 if d else 1), device_id_type=MESH)
    pl.semaphore_wait(barrier, count)

    def remote(src, dst, send, recv, to):
        copy = pltpu.make_async_remote_copy(
            src_ref=src, dst_ref=dst, send_sem=send, recv_sem=recv,
            device_id=to, device_id_type=MESH,
        )
        copy.start()
        return copy

    tail, head = pl.ds(length - MARGIN, MARGIN), pl.ds(0, MARGIN)
    halos = [
        remote(cur_ref.at[tail], prev_ref, hsend.at[0], hrecv.at[0], device(1, 0)),
        remote(cur_ref.at[head], next_ref, hsend.at[1], hrecv.at[1], device(count - 1, 0)),
        remote(cot_ref.at[tail], cprev_ref, hsend.at[2], hrecv.at[2], device(1, 0)),
        remote(cot_ref.at[head], cnext_ref, hsend.at[3], hrecv.at[3], device(count - 1, 0)),
    ]
    for copy in halos:
        copy.wait()
    has_prev = jnp.where(me > 0, 1.0, 0.0).astype(F32)
    has_next = jnp.where(me < count - 1, 1.0, 0.0).astype(F32)
    corr_ref[...] = jnp.zeros_like(corr_ref)

    def group(g, carry):
        def cols(s):
            return pl.ds(pl.multiple_of(s * width + g * GW, GW), GW)

        own = cols(0)

        def rows3(a, b, c, s):
            return (
                a[:, cols(s)].astype(F32) * has_prev,
                b[:, cols(s)].astype(F32),
                c[:, cols(s)].astype(F32) * has_next,
            )

        def fill(buf, parts):
            buf[0:MARGIN, :] = parts[0]
            buf[MARGIN:MARGIN + length, :] = parts[1]
            buf[MARGIN + length:, :] = parts[2]

        cots = rows3(cprev_ref, cot_ref, cnext_ref, 0)
        fill(si, rows3(prev_ref, cur_ref, next_ref, 0))
        fill(li, rows3(prev_ref, cur_ref, next_ref, 1))
        sgate = rows3(prev_ref, cur_ref, next_ref, 2)
        lgate = rows3(prev_ref, cur_ref, next_ref, 3)
        sgrad = [c * v for c, v in zip(cots, sgate)]
        lgrad = [rounded(c * v) for c, v in zip(cots, lgate)]
        fill(gs, sgrad)
        fill(gl, lgrad)
        fd, md = fd_ref[g], md_ref[g]
        cot = cots[1]
        short_out = jnp.zeros((length, GW), F32)
        d_short = jnp.zeros((length, GW), F32)
        for t in range(7):
            tap = tied_ref[t:t + 1, own]
            view = si[MARGIN + t - 3:MARGIN + t - 3 + length, :]
            short_out += tap * view
            corr_ref[t:t + 1, own] = jnp.sum(sgrad[1] * view, axis=0, keepdims=True)
            d_short += tap * gs[MARGIN - t + 3:MARGIN - t + 3 + length, :]
        fwd = jnp.zeros((length, GW), F32)
        bwd = jnp.zeros((length, GW), F32)
        mir = jnp.zeros((length, GW), F32)
        mirb = jnp.zeros((length, GW), F32)
        for t in range(5):
            kf = kf_ref[t:t + 1, own]
            km = km_ref[t:t + 1, own]
            view = li[pl.ds(MARGIN + (t - 2) * fd, length), :]
            fwd += kf * view
            corr_ref[7 + t:8 + t, own] = jnp.sum(lgrad[1] * view, axis=0, keepdims=True)
            view = li[pl.ds(MARGIN - (t - 2) * md, length), :]
            mir += km * view
            corr_ref[12 + t:13 + t, own] = jnp.sum(lgrad[1] * view, axis=0, keepdims=True)
            bwd += kf * gl[pl.ds(MARGIN - (t - 2) * fd, length), :]
            mirb += km * gl[pl.ds(MARGIN + (t - 2) * md, length), :]
        long_out = fwd + rounded(mir)
        out_ref[:, own] = (
            hid_ref[:, own].astype(F32) + sgate[1] * short_out + lgate[1] * long_out
        ).astype(BF16)
        stack[chan, :, cols(0)] = d_short.astype(BF16)
        stack[chan, :, cols(1)] = (bwd + rounded(mirb)).astype(BF16)
        stack[chan, :, cols(2)] = (cot * short_out).astype(BF16)
        stack[chan, :, cols(3)] = (cot * long_out).astype(BF16)
        return carry

    lax.fori_loop(0, width // GW, group, 0)
    swapped = remote(stack.at[chan], stack.at[chan], psend.at[0], precv.at[0], device(0, 1))
    sends = []
    for d in range(1, count):
        at = pl.multiple_of(lax.rem(me + d, count) * cw, GW)
        sends.append(
            remote(stack.at[chan, :, pl.ds(at, cw)], landed.at[me], asend.at[d], arecv.at[d],
                   device(d, 0))
        )
    landed[me] = stack[chan, :, pl.ds(pl.multiple_of(me * cw, GW), cw)]
    load.wait()
    swapped.wait()
    step = 2 * GW

    def back(i, carry):
        at = pl.ds(pl.multiple_of(i * step, step), step)
        term = mm_t(stack[...].reshape(2 * length, 4 * width), wbuf[at, :])
        near_ref[:, at] = term[:length]
        far[:, at] = term[length:].astype(BF16)
        return carry

    lax.fori_loop(0, width // step, back, 0)
    crossed = remote(far, got, psend.at[1], precv.at[1], device(0, 1))
    crossed.wait()
    got_ref[...] = got[...]
    for copy in sends:
        copy.wait()
    col_ref[...] = landed[...]


def sum_kernel(count, x_ref, o_ref, got, mine, full, ssem, rsem, bssem, brsem):
    me = lax.axis_index("seq")
    chan = lax.axis_index("chan")
    part = lax.axis_index("groups")
    peers = [(d, c) for d in range(count) for c in range(2) if d or c]

    def device(d, c):
        return (part, lax.rem(me + d, count), lax.rem(chan + c, 2))

    barrier = pltpu.get_barrier_semaphore()
    for d, c in peers:
        pl.semaphore_signal(barrier, inc=1, device_id=device(d, c), device_id_type=MESH)
    pl.semaphore_wait(barrier, len(peers))
    sends = []
    for d in range(1, count):
        copy = pltpu.make_async_remote_copy(
            src_ref=x_ref.at[lax.rem(me + d, count)],
            dst_ref=got.at[d],
            send_sem=ssem.at[d],
            recv_sem=rsem.at[d],
            device_id=device(d, 0),
            device_id_type=MESH,
        )
        copy.start()
        sends.append(copy)
    total = x_ref[me]
    for d in range(1, count):
        sends[d - 1].wait_recv()
        total = total + got[d]
    mine[...] = total
    casts = []
    for d, c in peers:
        copy = pltpu.make_async_remote_copy(
            src_ref=mine,
            dst_ref=full.at[chan, me],
            send_sem=bssem.at[d, c],
            recv_sem=brsem.at[d, c],
            device_id=device(d, c),
            device_id_type=MESH,
        )
        copy.start()
        casts.append(copy)
    full[chan, me] = total
    for copy in casts:
        copy.wait_recv()
    o_ref[...] = full[...]
    for copy in sends + casts:
        copy.wait_send()


def vmem():
    return pl.BlockSpec(memory_space=pltpu.VMEM)


def smem():
    return pl.BlockSpec(memory_space=pltpu.SMEM)


def all_sum(values, count):
    rows, width = values.shape
    lines = rows * width // (count * 128)
    x = values.reshape(count, lines, 128)
    out = pl.pallas_call(
        functools.partial(sum_kernel, count),
        out_shape=jax.ShapeDtypeStruct((2, count, lines, 128), F32),
        in_specs=[vmem()],
        out_specs=vmem(),
        scratch_shapes=[
            pltpu.VMEM((count, lines, 128), F32),
            pltpu.VMEM((lines, 128), F32),
            pltpu.VMEM((2, count, lines, 128), F32),
            pltpu.SemaphoreType.DMA((count,)),
            pltpu.SemaphoreType.DMA((count,)),
            pltpu.SemaphoreType.DMA((count, 2)),
            pltpu.SemaphoreType.DMA((count, 2)),
        ],
        compiler_params=pltpu.CompilerParams(collective_id=0, has_side_effects=True),
        cost_estimate=pl.CostEstimate(flops=10**6, bytes_accessed=10**6, transcendentals=0),
    )(x)
    return out.reshape(2, rows, width)


def local(residual, index, table, weight, short_taps, long_taps, dilations, cotangent):
    length, width = residual.shape
    groups = width // GW
    count = lax.axis_size("seq")
    side = lax.axis_index("chan")
    me = lax.axis_index("seq")
    low = side == 0
    own_table = lax.dynamic_slice_in_dim(table, side * width, width, 1).astype(F32)
    picked = sum(jnp.where(index[:, None] == b, own_table[b:b + 1], 0.0) for b in range(4))
    hidden = (residual.astype(F32) + picked).astype(BF16)

    at = jnp.arange(width, dtype=jnp.int32)
    total = at[:, None] + at[None, :]
    anti = total == width - 1
    turn = anti.astype(BF16)
    order = jnp.where(low, at[:, None] == at[None, :], anti).astype(BF16)

    short_low, short_high = short_taps[:, :width], short_taps[:, ::-1][:, :width]
    tied = jnp.where(low, short_low + short_high[::-1], short_high + short_low[::-1])
    long_low, long_high = long_taps[:, :width], long_taps[:, ::-1][:, :width]
    kf, km = jnp.where(low, long_low, long_high), jnp.where(low, long_high, long_low)
    dil_low, dil_high = dilations[:groups], dilations[::-1][:groups]
    fd, md = jnp.where(low, dil_low, dil_high), jnp.where(low, dil_high, dil_low)

    cot = mm(cotangent, order).astype(BF16)
    all_hidden = lax.all_gather(hidden, "seq", axis=0, tiled=True)

    turned = mm(swap(hidden), turn).astype(BF16)
    hid = mm(hidden, order).astype(BF16)
    far = mm(jnp.where(low, turned, hidden), weight).astype(BF16)
    near = mm(jnp.where(low, hidden, turned), weight)
    streams = (near + swap(far).astype(F32)).astype(BF16)

    cw = weight.shape[1] // count
    span = length + 2 * MARGIN
    block, corr, near, far, col_sg = pl.pallas_call(
        functools.partial(seq_kernel, count),
        out_shape=(
            jax.ShapeDtypeStruct((length, width), BF16),
            jax.ShapeDtypeStruct((17, width), F32),
            jax.ShapeDtypeStruct((length, width), F32),
            jax.ShapeDtypeStruct((length, width), BF16),
            jax.ShapeDtypeStruct((count, length, cw), BF16),
        ),
        in_specs=[smem()] * 2 + [vmem()] * 6 + [pl.BlockSpec(memory_space=pl.ANY)],
        out_specs=(vmem(),) * 5,
        scratch_shapes=[pltpu.VMEM((span, GW), F32)] * 4
        + [pltpu.VMEM((MARGIN, 4 * width), BF16)] * 2
        + [pltpu.VMEM((MARGIN, width), BF16)] * 2
        + [
            pltpu.VMEM((2, length, 4 * width), BF16),
            pltpu.VMEM((width, 4 * width), BF16),
            pltpu.VMEM((length, width), BF16),
            pltpu.VMEM((length, width), BF16),
            pltpu.VMEM((count, length, cw), BF16),
            pltpu.SemaphoreType.DMA,
            pltpu.SemaphoreType.DMA((4,)),
            pltpu.SemaphoreType.DMA((4,)),
            pltpu.SemaphoreType.DMA((count,)),
            pltpu.SemaphoreType.DMA((count,)),
            pltpu.SemaphoreType.DMA((2,)),
            pltpu.SemaphoreType.DMA((2,)),
        ],
        compiler_params=pltpu.CompilerParams(
            vmem_limit_bytes=40 * 2**20, collective_id=1, has_side_effects=True
        ),
        cost_estimate=pl.CostEstimate(
            flops=3 * 10**9, bytes_accessed=5 * 10**7, transcendentals=0
        ),
    )(fd, md, tied, kf, km, streams, cot, hid, weight)
    block_result_output = mm(block, order).astype(BF16)
    hidden_input_gradient = cotangent.astype(F32) + near + mm(far, turn)

    embedding = jnp.stack(
        [
            jnp.sum(jnp.where(index[:, None] == b, hidden_input_gradient, 0.0), axis=0)
            for b in range(4)
        ]
    )
    small = jnp.concatenate([corr, embedding, jnp.zeros((3, width), F32)], axis=0)
    summed = all_sum(small, count)

    all_turned = mm(swap(all_hidden), turn).astype(BF16)
    col_sg = col_sg.reshape(count * length, cw)
    other = swap(col_sg)
    rows = (((0,), (0,)), ((), ()))
    mixing_half_gradient = lax.dot_general(
        all_hidden, jnp.where(low, col_sg, other), rows, preferred_element_type=F32
    ) + lax.dot_general(
        all_turned, jnp.where(low, other, col_sg), rows, preferred_element_type=F32
    )

    a, b = summed[0], summed[1]
    tied_sum = a[0:7] + b[0:7][::-1]
    short_kernel_gradient = jnp.concatenate([tied_sum, tied_sum[::-1, ::-1]], axis=1)
    dilated_kernel_gradient = jnp.concatenate(
        [a[7:12] + b[12:17], (b[7:12] + a[12:17])[:, ::-1]], axis=1
    )
    embedding_table_gradient = jnp.concatenate([a[17:21], b[17:21]], axis=1)
    return (
        block_result_output,
        hidden_input_gradient,
        mixing_half_gradient,
        embedding_table_gradient,
        short_kernel_gradient,
        dilated_kernel_gradient,
    )


def solution(mesh):
    placed = (
        P(("groups", "seq"), "chan"),
        P(("groups", "seq")),
        P(),
        P("chan", None),
        P(),
        P(),
        P(),
        P(("groups", "seq"), "chan"),
    )
    return jax.shard_map(
        local,
        mesh=mesh,
        in_specs=placed,
        out_specs=(
            P(("groups", "seq"), "chan"),
            P(("groups", "seq"), "chan"),
            P(("groups", "chan"), "seq"),
            P("groups", None),
            P("groups", None),
            P("groups", None),
        ),
        check_vma=False,
    )
```

```python
import functools

import jax
import jax.numpy as jnp
from jax import lax
from jax.experimental import pallas as pl
from jax.experimental.pallas import tpu as pltpu
from jax.sharding import PartitionSpec as P

GW = 128
DMAX = 16
MARGIN = 2 * DMAX
F32 = jnp.float32
BF16 = jnp.bfloat16
MESH = pl.DeviceIdType.MESH


def swap(value):
    return lax.ppermute(value, "chan", [(0, 1), (1, 0)])


def mm(a, b):
    return jnp.dot(a, b, preferred_element_type=F32)


def mm_t(a, b):
    return lax.dot_general(a, b, (((1,), (1,)), ((), ())), preferred_element_type=F32)


def rounded(v):
    return v.astype(BF16).astype(F32)


def seq_kernel(count, fd_ref, md_ref, tied_ref, kf_ref, km_ref, cur_ref, cot_ref, hid_ref, cotn_ref, hot_ref, w_ref,
               out_ref, sum_ref, near_ref, got_ref, col_ref, si, li, gs, gl, prev_ref, next_ref,
               cprev_ref, cnext_ref, stack, wbuf, far, got, landed, wsem, hsend, hrecv, asend,
               arecv, psend, precv, small, parts, mine, full, ssend, srecv, bsend, brecv):
    length, width = cot_ref.shape
    cw = 4 * width // count
    me = lax.axis_index("seq")
    chan = lax.axis_index("chan")
    part = lax.axis_index("groups")
    load = pltpu.make_async_copy(w_ref, wbuf, wsem)
    load.start()

    def device(d, c):
        return (part, lax.rem(me + d, count), lax.rem(chan + c, 2))

    barrier = pltpu.get_barrier_semaphore()
    peers = [(d, c) for d in range(count) for c in range(2) if d or c]
    for d, c in peers:
        pl.semaphore_signal(barrier, inc=1, device_id=device(d, c), device_id_type=MESH)
    pl.semaphore_wait(barrier, len(peers))

    def remote(src, dst, send, recv, to):
        copy = pltpu.make_async_remote_copy(
            src_ref=src, dst_ref=dst, send_sem=send, recv_sem=recv,
            device_id=to, device_id_type=MESH,
        )
        copy.start()
        return copy

    tail, head = pl.ds(length - MARGIN, MARGIN), pl.ds(0, MARGIN)
    halos = [
        remote(cur_ref.at[tail], prev_ref, hsend.at[0], hrecv.at[0], device(1, 0)),
        remote(cur_ref.at[head], next_ref, hsend.at[1], hrecv.at[1], device(count - 1, 0)),
        remote(cot_ref.at[tail], cprev_ref, hsend.at[2], hrecv.at[2], device(1, 0)),
        remote(cot_ref.at[head], cnext_ref, hsend.at[3], hrecv.at[3], device(count - 1, 0)),
    ]
    for copy in halos:
        copy.wait()
    has_prev = jnp.where(me > 0, 1.0, 0.0).astype(F32)
    has_next = jnp.where(me < count - 1, 1.0, 0.0).astype(F32)
    small[...] = jnp.zeros_like(small)

    def group(g, carry):
        def cols(s):
            return pl.ds(pl.multiple_of(s * width + g * GW, GW), GW)

        own = cols(0)

        def rows3(a, b, c, s):
            return (
                a[:, cols(s)].astype(F32) * has_prev,
                b[:, cols(s)].astype(F32),
                c[:, cols(s)].astype(F32) * has_next,
            )

        def fill(buf, parts):
            buf[0:MARGIN, :] = parts[0]
            buf[MARGIN:MARGIN + length, :] = parts[1]
            buf[MARGIN + length:, :] = parts[2]

        cots = rows3(cprev_ref, cot_ref, cnext_ref, 0)
        fill(si, rows3(prev_ref, cur_ref, next_ref, 0))
        fill(li, rows3(prev_ref, cur_ref, next_ref, 1))
        sgate = rows3(prev_ref, cur_ref, next_ref, 2)
        lgate = rows3(prev_ref, cur_ref, next_ref, 3)
        sgrad = [c * v for c, v in zip(cots, sgate)]
        lgrad = [rounded(c * v) for c, v in zip(cots, lgate)]
        fill(gs, sgrad)
        fill(gl, lgrad)
        fd, md = fd_ref[g], md_ref[g]
        cot = cots[1]
        short_out = jnp.zeros((length, GW), F32)
        d_short = jnp.zeros((length, GW), F32)
        for t in range(7):
            tap = tied_ref[t:t + 1, own]
            view = si[MARGIN + t - 3:MARGIN + t - 3 + length, :]
            short_out += tap * view
            small[t, pl.ds(g, 1), :] = jnp.sum(sgrad[1] * view, axis=0, keepdims=True)
            d_short += tap * gs[MARGIN - t + 3:MARGIN - t + 3 + length, :]
        fwd = jnp.zeros((length, GW), F32)
        bwd = jnp.zeros((length, GW), F32)
        mir = jnp.zeros((length, GW), F32)
        mirb = jnp.zeros((length, GW), F32)
        for t in range(5):
            kf = kf_ref[t:t + 1, own]
            km = km_ref[t:t + 1, own]
            view = li[pl.ds(MARGIN + (t - 2) * fd, length), :]
            fwd += kf * view
            small[7 + t, pl.ds(g, 1), :] = jnp.sum(lgrad[1] * view, axis=0, keepdims=True)
            view = li[pl.ds(MARGIN - (t - 2) * md, length), :]
            mir += km * view
            small[12 + t, pl.ds(g, 1), :] = jnp.sum(lgrad[1] * view, axis=0, keepdims=True)
            bwd += kf * gl[pl.ds(MARGIN - (t - 2) * fd, length), :]
            mirb += km * gl[pl.ds(MARGIN + (t - 2) * md, length), :]
        long_out = fwd + rounded(mir)
        out_ref[:, own] = (
            hid_ref[:, own].astype(F32) + sgate[1] * short_out + lgate[1] * long_out
        ).astype(BF16)
        stack[chan, :, cols(0)] = d_short.astype(BF16)
        stack[chan, :, cols(1)] = (bwd + rounded(mirb)).astype(BF16)
        stack[chan, :, cols(2)] = (cot * short_out).astype(BF16)
        stack[chan, :, cols(3)] = (cot * long_out).astype(BF16)
        return carry

    lax.fori_loop(0, width // GW, group, 0)
    swapped = remote(stack.at[chan], stack.at[chan], psend.at[0], precv.at[0], device(0, 1))
    sends = []
    for d in range(1, count):
        at = pl.multiple_of(lax.rem(me + d, count) * cw, GW)
        sends.append(
            remote(stack.at[chan, :, pl.ds(at, cw)], landed.at[me], asend.at[d], arecv.at[d],
                   device(d, 0))
        )
    landed[me] = stack[chan, :, pl.ds(pl.multiple_of(me * cw, GW), cw)]
    load.wait()
    swapped.wait()
    step = 2 * GW

    def back(i, carry):
        at = pl.ds(pl.multiple_of(i * step, step), step)
        term = mm_t(stack[...].reshape(2 * length, 4 * width), wbuf[at, :])
        near_ref[:, at] = term[:length]
        far[:, at] = term[length:].astype(BF16)
        return carry

    lax.fori_loop(0, width // step, back, 0)
    crossed = remote(far, got, psend.at[1], precv.at[1], device(0, 1))
    crossed.wait()
    got_ref[...] = got[...]

    hot = hot_ref[...]
    rest = cotn_ref[...].astype(F32) + near_ref[...]
    table = jnp.zeros((hot.shape[0], width), F32)
    for _ in range(3):
        piece = rest.astype(BF16)
        table += mm(hot, piece)
        rest = rest - piece.astype(F32)
    turned = mm(hot, got[...])
    for i in range(width // GW):
        for b in range(4):
            at = slice(i * GW, (i + 1) * GW)
            small[17 + b, i:i + 1, :] = table[b:b + 1, at]
            small[21 + b, i:i + 1, :] = turned[b:b + 1, at]

    share = small.shape[0] // count
    shares = []
    for d in range(1, count):
        at = pl.ds(lax.rem(me + d, count) * share, share)
        shares.append(remote(small.at[at], parts.at[d], ssend.at[d], srecv.at[d], device(d, 0)))
    own_rows = pl.ds(me * share, share)
    total = small[own_rows]
    for d in range(1, count):
        shares[d - 1].wait_recv()
        total = total + parts[d]
    mine[...] = total
    casts = [
        remote(mine, full.at[chan, own_rows], bsend.at[d, c], brecv.at[d, c], device(d, c))
        for d, c in peers
    ]
    full[chan, own_rows] = total
    for copy in casts:
        copy.wait()
    for copy in shares:
        copy.wait_send()
    sum_ref[...] = full[...]
    for copy in sends:
        copy.wait()
    col_ref[...] = landed[...]


def vmem():
    return pl.BlockSpec(memory_space=pltpu.VMEM)


def smem():
    return pl.BlockSpec(memory_space=pltpu.SMEM)


def local(residual, index, table, weight, short_taps, long_taps, dilations, cotangent):
    length, width = residual.shape
    groups = width // GW
    count = lax.axis_size("seq")
    side = lax.axis_index("chan")
    me = lax.axis_index("seq")
    low = side == 0
    own_table = lax.dynamic_slice_in_dim(table, side * width, width, 1).astype(F32)
    picked = sum(jnp.where(index[:, None] == b, own_table[b:b + 1], 0.0) for b in range(4))
    hidden = (residual.astype(F32) + picked).astype(BF16)

    at = jnp.arange(width, dtype=jnp.int32)
    total = at[:, None] + at[None, :]
    anti = total == width - 1
    turn = anti.astype(BF16)
    order = jnp.where(low, at[:, None] == at[None, :], anti).astype(BF16)

    short_low, short_high = short_taps[:, :width], short_taps[:, ::-1][:, :width]
    tied = jnp.where(low, short_low + short_high[::-1], short_high + short_low[::-1])
    long_low, long_high = long_taps[:, :width], long_taps[:, ::-1][:, :width]
    kf, km = jnp.where(low, long_low, long_high), jnp.where(low, long_high, long_low)
    dil_low, dil_high = dilations[:groups], dilations[::-1][:groups]
    fd, md = jnp.where(low, dil_low, dil_high), jnp.where(low, dil_high, dil_low)

    cot = mm(cotangent, order).astype(BF16)
    all_hidden = lax.all_gather(hidden, "seq", axis=0, tiled=True)

    turned = mm(swap(hidden), turn).astype(BF16)
    hid = mm(hidden, order).astype(BF16)
    far = mm(jnp.where(low, turned, hidden), weight).astype(BF16)
    near = mm(jnp.where(low, hidden, turned), weight)
    streams = (near + swap(far).astype(F32)).astype(BF16)

    hot = (jnp.arange(16, dtype=jnp.int32)[:, None] == index[None, :]).astype(BF16)
    cw = weight.shape[1] // count
    span = length + 2 * MARGIN
    block, summed, near, far, col_sg = pl.pallas_call(
        functools.partial(seq_kernel, count),
        out_shape=(
            jax.ShapeDtypeStruct((length, width), BF16),
            jax.ShapeDtypeStruct((2, 32, groups, GW), F32),
            jax.ShapeDtypeStruct((length, width), F32),
            jax.ShapeDtypeStruct((length, width), BF16),
            jax.ShapeDtypeStruct((count, length, cw), BF16),
        ),
        in_specs=[smem()] * 2 + [vmem()] * 8 + [pl.BlockSpec(memory_space=pl.ANY)],
        out_specs=(vmem(),) * 5,
        scratch_shapes=[pltpu.VMEM((span, GW), F32)] * 4
        + [pltpu.VMEM((MARGIN, 4 * width), BF16)] * 2
        + [pltpu.VMEM((MARGIN, width), BF16)] * 2
        + [
            pltpu.VMEM((2, length, 4 * width), BF16),
            pltpu.VMEM((width, 4 * width), BF16),
            pltpu.VMEM((length, width), BF16),
            pltpu.VMEM((length, width), BF16),
            pltpu.VMEM((count, length, cw), BF16),
            pltpu.SemaphoreType.DMA,
            pltpu.SemaphoreType.DMA((4,)),
            pltpu.SemaphoreType.DMA((4,)),
            pltpu.SemaphoreType.DMA((count,)),
            pltpu.SemaphoreType.DMA((count,)),
            pltpu.SemaphoreType.DMA((2,)),
            pltpu.SemaphoreType.DMA((2,)),
            pltpu.VMEM((32, groups, GW), F32),
            pltpu.VMEM((count, 32 // count, groups, GW), F32),
            pltpu.VMEM((32 // count, groups, GW), F32),
            pltpu.VMEM((2, 32, groups, GW), F32),
            pltpu.SemaphoreType.DMA((count,)),
            pltpu.SemaphoreType.DMA((count,)),
            pltpu.SemaphoreType.DMA((count, 2)),
            pltpu.SemaphoreType.DMA((count, 2)),
        ],
        compiler_params=pltpu.CompilerParams(
            vmem_limit_bytes=40 * 2**20, collective_id=1, has_side_effects=True
        ),
        cost_estimate=pl.CostEstimate(
            flops=3 * 10**9, bytes_accessed=5 * 10**7, transcendentals=0
        ),
    )(fd, md, tied, kf, km, streams, cot, hid, cotangent, hot, weight)
    block_result_output = mm(block, order).astype(BF16)
    hidden_input_gradient = cotangent.astype(F32) + near + mm(far, turn)

    summed = summed.reshape(2, 32, width)
    all_turned = mm(swap(all_hidden), turn).astype(BF16)
    col_sg = col_sg.reshape(count * length, cw)
    other = swap(col_sg)
    rows = (((0,), (0,)), ((), ()))
    mixing_half_gradient = lax.dot_general(
        all_hidden, jnp.where(low, col_sg, other), rows, preferred_element_type=F32
    ) + lax.dot_general(
        all_turned, jnp.where(low, other, col_sg), rows, preferred_element_type=F32
    )

    a, b = summed[0], summed[1]
    tied_sum = a[0:7] + b[0:7][::-1]
    short_kernel_gradient = jnp.concatenate([tied_sum, tied_sum[::-1, ::-1]], axis=1)
    dilated_kernel_gradient = jnp.concatenate(
        [a[7:12] + b[12:17], (b[7:12] + a[12:17])[:, ::-1]], axis=1
    )
    embedding_table_gradient = jnp.concatenate(
        [a[17:21] + a[21:25, ::-1], b[17:21] + b[21:25, ::-1]], axis=1
    )
    return (
        block_result_output,
        hidden_input_gradient,
        mixing_half_gradient,
        embedding_table_gradient,
        short_kernel_gradient,
        dilated_kernel_gradient,
    )


def solution(mesh):
    placed = (
        P(("groups", "seq"), "chan"),
        P(("groups", "seq")),
        P(),
        P("chan", None),
        P(),
        P(),
        P(),
        P(("groups", "seq"), "chan"),
    )
    return jax.shard_map(
        local,
        mesh=mesh,
        in_specs=placed,
        out_specs=(
            P(("groups", "seq"), "chan"),
            P(("groups", "seq"), "chan"),
            P(("groups", "chan"), "seq"),
            P("groups", None),
            P("groups", None),
            P("groups", None),
        ),
        check_vma=False,
    )
```

```python
import functools

import jax
import jax.numpy as jnp
from jax import lax
from jax.experimental import pallas as pl
from jax.experimental.pallas import tpu as pltpu
from jax.sharding import PartitionSpec as P

GW = 128
DMAX = 16
MARGIN = 2 * DMAX
F32 = jnp.float32
BF16 = jnp.bfloat16
MESH = pl.DeviceIdType.MESH


def swap(value):
    return lax.ppermute(value, "chan", [(0, 1), (1, 0)])


def mm(a, b):
    return jnp.dot(a, b, preferred_element_type=F32)


def mm_t(a, b):
    return lax.dot_general(a, b, (((1,), (1,)), ((), ())), preferred_element_type=F32)


def rounded(v):
    return v.astype(BF16).astype(F32)


def seq_kernel(count, fd_ref, md_ref, tied_ref, kf_ref, km_ref, cur_ref, cot_ref, hid_ref, cotn_ref, hot_ref, w_ref,
               out_ref, sum_ref, near_ref, got_ref, col_ref, si, li, gs, gl, prev_ref, next_ref,
               cprev_ref, cnext_ref, stack, wbuf, far, got, landed, wsem, hsend, hrecv, asend,
               arecv, psend, precv, small, parts, mine, full, ssend, srecv, bsend, brecv):
    length, width = cot_ref.shape
    cw = 4 * width // count
    me = lax.axis_index("seq")
    chan = lax.axis_index("chan")
    part = lax.axis_index("groups")
    load = pltpu.make_async_copy(w_ref, wbuf, wsem)
    load.start()

    def device(d, c):
        return (part, lax.rem(me + d, count), lax.rem(chan + c, 2))

    barrier = pltpu.get_barrier_semaphore()
    peers = [(d, c) for d in range(count) for c in range(2) if d or c]
    for d, c in peers:
        pl.semaphore_signal(barrier, inc=1, device_id=device(d, c), device_id_type=MESH)
    pl.semaphore_wait(barrier, len(peers))

    def remote(src, dst, send, recv, to):
        copy = pltpu.make_async_remote_copy(
            src_ref=src, dst_ref=dst, send_sem=send, recv_sem=recv,
            device_id=to, device_id_type=MESH,
        )
        copy.start()
        return copy

    tail, head = pl.ds(length - MARGIN, MARGIN), pl.ds(0, MARGIN)
    halos = [
        remote(cur_ref.at[tail], prev_ref, hsend.at[0], hrecv.at[0], device(1, 0)),
        remote(cur_ref.at[head], next_ref, hsend.at[1], hrecv.at[1], device(count - 1, 0)),
        remote(cot_ref.at[tail], cprev_ref, hsend.at[2], hrecv.at[2], device(1, 0)),
        remote(cot_ref.at[head], cnext_ref, hsend.at[3], hrecv.at[3], device(count - 1, 0)),
    ]
    for copy in halos:
        copy.wait()
    has_prev = jnp.where(me > 0, 1.0, 0.0).astype(F32)
    has_next = jnp.where(me < count - 1, 1.0, 0.0).astype(F32)
    small[...] = jnp.zeros_like(small)

    def group(g, carry):
        def cols(s):
            return pl.ds(pl.multiple_of(s * width + g * GW, GW), GW)

        own = cols(0)

        def rows3(a, b, c, s):
            return (
                a[:, cols(s)].astype(F32) * has_prev,
                b[:, cols(s)].astype(F32),
                c[:, cols(s)].astype(F32) * has_next,
            )

        def fill(buf, parts):
            buf[0:MARGIN, :] = parts[0]
            buf[MARGIN:MARGIN + length, :] = parts[1]
            buf[MARGIN + length:, :] = parts[2]

        cots = rows3(cprev_ref, cot_ref, cnext_ref, 0)
        fill(si, rows3(prev_ref, cur_ref, next_ref, 0))
        fill(li, rows3(prev_ref, cur_ref, next_ref, 1))
        sgate = rows3(prev_ref, cur_ref, next_ref, 2)
        lgate = rows3(prev_ref, cur_ref, next_ref, 3)
        sgrad = [c * v for c, v in zip(cots, sgate)]
        lgrad = [rounded(c * v) for c, v in zip(cots, lgate)]
        fill(gs, sgrad)
        fill(gl, lgrad)
        fd, md = fd_ref[g], md_ref[g]
        cot = cots[1]
        short_out = jnp.zeros((length, GW), F32)
        d_short = jnp.zeros((length, GW), F32)
        for t in range(7):
            tap = tied_ref[t:t + 1, own]
            view = si[MARGIN + t - 3:MARGIN + t - 3 + length, :]
            short_out += tap * view
            small[t, pl.ds(g, 1), :] = jnp.sum(sgrad[1] * view, axis=0, keepdims=True)
            d_short += tap * gs[MARGIN - t + 3:MARGIN - t + 3 + length, :]
        fwd = jnp.zeros((length, GW), F32)
        bwd = jnp.zeros((length, GW), F32)
        mir = jnp.zeros((length, GW), F32)
        mirb = jnp.zeros((length, GW), F32)
        for t in range(5):
            kf = kf_ref[t:t + 1, own]
            km = km_ref[t:t + 1, own]
            view = li[pl.ds(MARGIN + (t - 2) * fd, length), :]
            fwd += kf * view
            small[7 + t, pl.ds(g, 1), :] = jnp.sum(lgrad[1] * view, axis=0, keepdims=True)
            view = li[pl.ds(MARGIN - (t - 2) * md, length), :]
            mir += km * view
            small[12 + t, pl.ds(g, 1), :] = jnp.sum(lgrad[1] * view, axis=0, keepdims=True)
            bwd += kf * gl[pl.ds(MARGIN - (t - 2) * fd, length), :]
            mirb += km * gl[pl.ds(MARGIN + (t - 2) * md, length), :]
        long_out = fwd + rounded(mir)
        out_ref[:, own] = (
            hid_ref[:, own].astype(F32) + sgate[1] * short_out + lgate[1] * long_out
        ).astype(BF16)
        stack[chan, :, cols(0)] = d_short.astype(BF16)
        stack[chan, :, cols(1)] = (bwd + rounded(mirb)).astype(BF16)
        stack[chan, :, cols(2)] = (cot * short_out).astype(BF16)
        stack[chan, :, cols(3)] = (cot * long_out).astype(BF16)
        return carry

    lax.fori_loop(0, width // GW, group, 0)
    swapped = remote(stack.at[chan], stack.at[chan], psend.at[0], precv.at[0], device(0, 1))
    sends = []
    for d in range(1, count):
        at = pl.multiple_of(lax.rem(me + d, count) * cw, GW)
        sends.append(
            remote(stack.at[chan, :, pl.ds(at, cw)], landed.at[me], asend.at[d], arecv.at[d],
                   device(d, 0))
        )
    landed[me] = stack[chan, :, pl.ds(pl.multiple_of(me * cw, GW), cw)]
    load.wait()
    swapped.wait()
    step = 2 * GW

    def back(i, carry):
        at = pl.ds(pl.multiple_of(i * step, step), step)
        term = mm_t(stack[...].reshape(2 * length, 4 * width), wbuf[at, :])
        near_ref[:, at] = term[:length]
        far[:, at] = term[length:].astype(BF16)
        return carry

    lax.fori_loop(0, width // step, back, 0)
    crossed = remote(far, got, psend.at[1], precv.at[1], device(0, 1))
    crossed.wait()
    got_ref[...] = got[...]

    hot = hot_ref[...]
    rest = cotn_ref[...].astype(F32) + near_ref[...]
    table = jnp.zeros((hot.shape[0], width), F32)
    for _ in range(3):
        piece = rest.astype(BF16)
        table += mm(hot, piece)
        rest = rest - piece.astype(F32)
    turned = mm(hot, got[...])
    for i in range(width // GW):
        for b in range(4):
            at = slice(i * GW, (i + 1) * GW)
            small[17 + b, i:i + 1, :] = table[b:b + 1, at]
            small[21 + b, i:i + 1, :] = turned[b:b + 1, at]

    share = small.shape[0] // count
    shares = []
    for d in range(1, count):
        at = pl.ds(lax.rem(me + d, count) * share, share)
        shares.append(remote(small.at[at], parts.at[d], ssend.at[d], srecv.at[d], device(d, 0)))
    own_rows = pl.ds(me * share, share)
    total = small[own_rows]
    for d in range(1, count):
        shares[d - 1].wait_recv()
        total = total + parts[d]
    mine[...] = total
    casts = [
        remote(mine, full.at[chan, own_rows], bsend.at[d, c], brecv.at[d, c], device(d, c))
        for d, c in peers
    ]
    full[chan, own_rows] = total
    for copy in casts:
        copy.wait()
    for copy in shares:
        copy.wait_send()
    sum_ref[...] = full[...]
    for copy in sends:
        copy.wait()
    col_ref[...] = landed[...]


def vmem():
    return pl.BlockSpec(memory_space=pltpu.VMEM)


def smem():
    return pl.BlockSpec(memory_space=pltpu.SMEM)


def local(residual, index, table, weight, short_taps, long_taps, dilations, cotangent):
    length, width = residual.shape
    groups = width // GW
    count = lax.axis_size("seq")
    side = lax.axis_index("chan")
    me = lax.axis_index("seq")
    low = side == 0
    own_table = lax.dynamic_slice_in_dim(table, side * width, width, 1).astype(F32)
    picked = sum(jnp.where(index[:, None] == b, own_table[b:b + 1], 0.0) for b in range(4))
    hidden = (residual.astype(F32) + picked).astype(BF16)

    at = jnp.arange(width, dtype=jnp.int32)
    total = at[:, None] + at[None, :]
    anti = total == width - 1
    turn = anti.astype(BF16)
    order = jnp.where(low, at[:, None] == at[None, :], anti).astype(BF16)

    short_low, short_high = short_taps[:, :width], short_taps[:, ::-1][:, :width]
    tied = jnp.where(low, short_low + short_high[::-1], short_high + short_low[::-1])
    long_low, long_high = long_taps[:, :width], long_taps[:, ::-1][:, :width]
    kf, km = jnp.where(low, long_low, long_high), jnp.where(low, long_high, long_low)
    dil_low, dil_high = dilations[:groups], dilations[::-1][:groups]
    fd, md = jnp.where(low, dil_low, dil_high), jnp.where(low, dil_high, dil_low)

    cot = mm(cotangent, order).astype(BF16)
    all_hidden = lax.all_gather(hidden, "seq", axis=0, tiled=True)

    turned = mm(swap(hidden), turn).astype(BF16)
    hid = mm(hidden, order).astype(BF16)
    both = mm(jnp.concatenate([hidden, turned], axis=0), weight)
    far = jnp.where(low, both[length:], both[:length]).astype(BF16)
    near = jnp.where(low, both[:length], both[length:])
    streams = (near + swap(far).astype(F32)).astype(BF16)

    hot = (jnp.arange(16, dtype=jnp.int32)[:, None] == index[None, :]).astype(BF16)
    cw = weight.shape[1] // count
    span = length + 2 * MARGIN
    block, summed, near, far, col_sg = pl.pallas_call(
        functools.partial(seq_kernel, count),
        out_shape=(
            jax.ShapeDtypeStruct((length, width), BF16),
            jax.ShapeDtypeStruct((2, 32, groups, GW), F32),
            jax.ShapeDtypeStruct((length, width), F32),
            jax.ShapeDtypeStruct((length, width), BF16),
            jax.ShapeDtypeStruct((count, length, cw), BF16),
        ),
        in_specs=[smem()] * 2 + [vmem()] * 8 + [pl.BlockSpec(memory_space=pl.ANY)],
        out_specs=(vmem(),) * 5,
        scratch_shapes=[pltpu.VMEM((span, GW), F32)] * 4
        + [pltpu.VMEM((MARGIN, 4 * width), BF16)] * 2
        + [pltpu.VMEM((MARGIN, width), BF16)] * 2
        + [
            pltpu.VMEM((2, length, 4 * width), BF16),
            pltpu.VMEM((width, 4 * width), BF16),
            pltpu.VMEM((length, width), BF16),
            pltpu.VMEM((length, width), BF16),
            pltpu.VMEM((count, length, cw), BF16),
            pltpu.SemaphoreType.DMA,
            pltpu.SemaphoreType.DMA((4,)),
            pltpu.SemaphoreType.DMA((4,)),
            pltpu.SemaphoreType.DMA((count,)),
            pltpu.SemaphoreType.DMA((count,)),
            pltpu.SemaphoreType.DMA((2,)),
            pltpu.SemaphoreType.DMA((2,)),
            pltpu.VMEM((32, groups, GW), F32),
            pltpu.VMEM((count, 32 // count, groups, GW), F32),
            pltpu.VMEM((32 // count, groups, GW), F32),
            pltpu.VMEM((2, 32, groups, GW), F32),
            pltpu.SemaphoreType.DMA((count,)),
            pltpu.SemaphoreType.DMA((count,)),
            pltpu.SemaphoreType.DMA((count, 2)),
            pltpu.SemaphoreType.DMA((count, 2)),
        ],
        compiler_params=pltpu.CompilerParams(
            vmem_limit_bytes=40 * 2**20, collective_id=1, has_side_effects=True
        ),
        cost_estimate=pl.CostEstimate(
            flops=3 * 10**9, bytes_accessed=5 * 10**7, transcendentals=0
        ),
    )(fd, md, tied, kf, km, streams, cot, hid, cotangent, hot, weight)
    block_result_output = mm(block, order).astype(BF16)
    hidden_input_gradient = cotangent.astype(F32) + near + mm(far, turn)

    summed = summed.reshape(2, 32, width)
    all_turned = mm(swap(all_hidden), turn).astype(BF16)
    col_sg = col_sg.reshape(count * length, cw)
    other = swap(col_sg)
    rows = (((0,), (0,)), ((), ()))
    mixing_half_gradient = lax.dot_general(
        all_hidden, jnp.where(low, col_sg, other), rows, preferred_element_type=F32
    ) + lax.dot_general(
        all_turned, jnp.where(low, other, col_sg), rows, preferred_element_type=F32
    )

    a, b = summed[0], summed[1]
    tied_sum = a[0:7] + b[0:7][::-1]
    short_kernel_gradient = jnp.concatenate([tied_sum, tied_sum[::-1, ::-1]], axis=1)
    dilated_kernel_gradient = jnp.concatenate(
        [a[7:12] + b[12:17], (b[7:12] + a[12:17])[:, ::-1]], axis=1
    )
    embedding_table_gradient = jnp.concatenate(
        [a[17:21] + a[21:25, ::-1], b[17:21] + b[21:25, ::-1]], axis=1
    )
    return (
        block_result_output,
        hidden_input_gradient,
        mixing_half_gradient,
        embedding_table_gradient,
        short_kernel_gradient,
        dilated_kernel_gradient,
    )


def solution(mesh):
    placed = (
        P(("groups", "seq"), "chan"),
        P(("groups", "seq")),
        P(),
        P("chan", None),
        P(),
        P(),
        P(),
        P(("groups", "seq"), "chan"),
    )
    return jax.shard_map(
        local,
        mesh=mesh,
        in_specs=placed,
        out_specs=(
            P(("groups", "seq"), "chan"),
            P(("groups", "seq"), "chan"),
            P(("groups", "chan"), "seq"),
            P("groups", None),
            P("groups", None),
            P("groups", None),
        ),
        check_vma=False,
    )
```
